768 devices in a mesh: col: 24 (over z, core), row: 4 (over x), rep: 8 (over y).
Axes of the slice: x: 4, y: 8, z: 12, core: 2. Of those that a mesh axis runs over, the one named last changes fastest.
Arguments:
- pooled_grad: bfloat16 [32, 3072, 48, 256], P(('row', 'rep'), 'col'), may hold values from -6 to 6
- giant_slot: int32 [24, 32, 3072, 8], P('col', ('row', 'rep')), may hold values from 0 to 2047, as said below
- touched_rows: int32 [24, 32, 32, 64], P('col', None, ('row', 'rep')), may hold values from 0 to 512, as said below
- bag_lengths: int32 [24, 32, 3072, 2], P('col', ('row', 'rep')), may hold values from 1 to 8, as said below
- small_ids: int32 [24, 32, 3072, 8], P('col', ('row', 'rep')), may hold values from 0 to 1023
- giant_weight: float32 [24, 16384, 256], P('col', ('row', 'rep')), may hold values from -4 to 4
- giant_accum: float32 [24, 16384], P('col', ('row', 'rep')), may hold values from 0.1 to 10
- small_weight: float32 [24, 1024, 256], P('col'), may hold values from -4 to 4
- small_accum: float32 [24, 1024], P('col'), may hold values from 0.1 to 10
Outputs:
- new_giant_weight: float32 [24, 16384, 256], P('col', ('row', 'rep'))
- new_giant_accum: float32 [24, 16384], P('col', ('row', 'rep'))
- new_small_weight: float32 [24, 1024, 256], P('col')
- new_small_accum: float32 [24, 1024], P('col')
The draws below stay inside these ranges and needn't reach their ends.
Inputs may be any that keep to these rules, and one draw needn't show every extreme that they name: touched_rows[c, s, d, :] holds local rows of shard d; its first entries are live and the rest equal 512; for each table one shard gets all 64 entries live from every source group, the block from group 0 to the last shard is full too, and every block has at least 16 live entries. giant_slot[c, s, j, k] = d * 64 + m names a live entry m of touched_rows[c, s, d, :]; the smallest and the largest value are taken in every draw. `bag_lengths`: in every sample group one sample uses all 8 positions for both tables.
All inputs are finite; a program needn't handle non-finite values.
Results may differ from the reference program's by a relative error of at most 0.0003.
Values may be sent and summed in bfloat16 or wider, within the bound.
No kernel may reach another device: no remote copies, remote signals or barrier semaphores. Data moves between devices by JAX's collectives and lax.ppermute only.
A program may use at most 64 MiB of HBM per device.

```python
import math
import jax
import jax.numpy as jnp
import numpy as np
from jax import lax

D = 256
BAG = 8
CAP = 64
G_DEV = 512
SMALL_ROWS = 1024
GROUPS = 32
TABLES = 48
SAMPLES_GRP = 3072
GIANT_ROWS = 16384
N_COL = 24


def hit_counts(key):
    key = jax.random.fold_in(key, 11)
    lower = jax.random.randint(key, (N_COL, GROUPS, GROUPS), CAP // 4, CAP + 1)
    hottest = jax.random.randint(jax.random.fold_in(key, 1), (N_COL, 1, 1), 0, GROUPS)
    owners = jnp.arange(GROUPS, dtype=jnp.int32)[None, None, :]
    counts = jnp.where(owners == hottest, CAP, lower)
    counts = counts.at[:, 0, GROUPS - 1].set(CAP)
    return counts.astype(jnp.int32)


def draw_touched_rows(key, part):
    counts = hit_counts(key)
    key = jax.random.fold_in(key, 3)
    first_row = jax.random.randint(key, (N_COL, GROUPS, GROUPS, 1), 0, G_DEV)
    stride = 2 * jax.random.randint(jax.random.fold_in(key, 1), (N_COL, GROUPS, GROUPS, 1), 0, max(G_DEV // 2, 1)) + 1
    position = jnp.arange(CAP, dtype=jnp.int32)[None, None, None, :]
    row_ids = (first_row + position * stride) % G_DEV
    return jnp.where(position < counts[..., None], row_ids, G_DEV).astype(jnp.int32)


def draw_giant_slot(key, part):
    counts = hit_counts(key)
    key = jax.random.fold_in(key, 5)
    shape = (N_COL, GROUPS, SAMPLES_GRP * BAG)
    owners = jax.random.randint(key, shape, 0, GROUPS)
    picks = jax.random.randint(jax.random.fold_in(key, 1), shape, 0, 1 << 20)
    limits = jnp.take_along_axis(counts, owners, axis=2)
    slot_ids = owners * CAP + picks % limits
    slot_ids = slot_ids.reshape(N_COL, GROUPS, SAMPLES_GRP, BAG)
    slot_ids = slot_ids.at[:, 0, 0, 0].set(GROUPS * CAP - 1)
    slot_ids = slot_ids.at[:, 0, 0, 1].set(0)
    return slot_ids.astype(jnp.int32)


def draw_bag_lengths(key, part):
    key = jax.random.fold_in(key, 7)
    lengths = jax.random.randint(key, (N_COL, GROUPS, SAMPLES_GRP, 2), 1, BAG + 1)
    leading = jnp.arange(SAMPLES_GRP, dtype=jnp.int32)[None, None, :, None] == 0
    return jnp.where(leading, BAG, lengths).astype(jnp.int32)


def place_ends(array, rng, smallest, top_value):
    place = [jax.random.randint(jax.random.fold_in(rng, axis), (), 0, length) for axis, length in enumerate(array.shape)]
    longest = array.shape.index(max(array.shape))
    next_to = place[:longest] + [(place[longest] + 1) % array.shape[longest]] + place[longest + 1:]
    return array.at[tuple(place)].set(smallest).at[tuple(next_to)].set(top_value)


def level_of(rng, dims, split, low, top_value):
    factor_of = 1.0
    for dim, parts in split:
        steps = jax.random.uniform(jax.random.fold_in(jax.random.fold_in(rng, 6), dim), (parts,), jnp.float32, low / len(split), top_value / len(split))
        factor_of = factor_of * jnp.repeat(jnp.exp(steps), dims[dim] // parts).reshape((-1,) + (1,) * (len(dims) - 1 - dim))
    return factor_of


def cumulative_ranks(number_of, skew):
    weights = [(1 << 20) // math.isqrt(standing ** skew) + 1 for standing in range(1, number_of + 1)]
    scale = 1 + sum(weights) // (1 << 30)
    return np.cumsum(np.array([max(1, weight // scale) for weight in weights]))


def ranked(stream_key, shape, amount, skew):
    listing = cumulative_ranks(amount, skew)
    lot = jax.random.randint(jax.random.fold_in(stream_key, 1), shape, 0, int(listing[amount - 1]))
    rank = jnp.searchsorted(jnp.asarray(listing, jnp.int32), lot, side="right")
    return jax.random.permutation(jax.random.fold_in(stream_key, 2), amount)[rank].astype(jnp.int32)


def centred(key, extent, scale, bound, shards=(), kind=jnp.bfloat16):
    factor_of = level_of(key, extent, shards, -0.22, 0.18) if shards else 1.0
    result = jax.random.normal(key, extent, jnp.float32) * scale * factor_of
    return jnp.minimum(jnp.maximum(result, -bound), bound).astype(kind)


def setup_inputs(seed: int = 0) -> dict:
    splits = jax.random.split(jax.random.key(seed), 10)
    return {
        "pooled_grad": centred(splits[0], (GROUPS, SAMPLES_GRP, TABLES, D), 1.0, 6.0, ((0, 32), (1, 24))),
        "giant_slot": draw_giant_slot(jax.random.fold_in(splits[9], 71), 0),
        "touched_rows": draw_touched_rows(jax.random.fold_in(splits[9], 71), 0),
        "bag_lengths": draw_bag_lengths(jax.random.fold_in(splits[9], 71), 0),
        "small_ids": place_ends(ranked(splits[4], (N_COL, GROUPS, SAMPLES_GRP, BAG), SMALL_ROWS, 2), jax.random.fold_in(splits[4], 3), 0, SMALL_ROWS - 1).astype(jnp.int32),
        "giant_weight": centred(splits[5], (N_COL, GIANT_ROWS, D), 0.3, 4.0, ((0, 24), (1, 32)), jnp.float32),
        "giant_accum": jnp.clip(jnp.exp(math.log(10.0) - 4.6051702 * jax.random.uniform(splits[6], (N_COL, GIANT_ROWS), jnp.float32) ** level_of(splits[6], (N_COL, GIANT_ROWS), ((0, 24), (1, 32)), -0.2, 0.2)), 0.1, 10.0),
        "small_weight": centred(splits[7], (N_COL, SMALL_ROWS, D), 0.3, 4.0, ((0, 24),), jnp.float32),
        "small_accum": jnp.clip(jnp.exp(math.log(10.0) - 4.6051702 * jax.random.uniform(splits[8], (N_COL, SMALL_ROWS), jnp.float32) ** level_of(splits[8], (N_COL, SMALL_ROWS), ((0, 24),), -0.2, 0.2)), 0.1, 10.0),
    }


LEARN = 0.5
TINY = 1e-08

def rowwise_adagrad(weight, accumulator, gradient):
    accumulator_new = accumulator + lax.optimization_barrier(jnp.mean(gradient * gradient, axis=-1))
    weight_new = weight - LEARN * gradient / (jnp.sqrt(accumulator_new)[..., None] + TINY)
    return (weight_new, accumulator_new)

def bag_sum(values, row_ids, lengths, bucket_count):
    is_live = jnp.arange(BAG, dtype=jnp.int32)[None, :] < lengths[:, None]
    target = jnp.where(is_live, row_ids, bucket_count)
    spread = jnp.broadcast_to(values.astype(jnp.float32)[:, None, :], (values.shape[0], BAG, values.shape[1]))
    empty = jnp.zeros((bucket_count, values.shape[1]), jnp.float32)
    return empty.at[target.reshape(-1)].add(spread.reshape(-1, values.shape[1]), mode='drop')

def reference(pooled_grad, giant_slot, touched_rows, bag_lengths, small_ids, giant_weight, giant_accum, small_weight, small_accum):

    def per_table(state, table_inputs):
        table_index, slot_ids, row_lists, length_table, small_table_ids, g_weight, g_accum, s_weight, s_accum = table_inputs
        giant_values = lax.dynamic_index_in_dim(pooled_grad, 2 * table_index, 2, keepdims=False)
        small_values = lax.dynamic_index_in_dim(pooled_grad, 2 * table_index + 1, 2, keepdims=False)

        def per_group(summed, group_inputs):
            g_values, s_values, g_ids, group_lengths, s_ids = group_inputs
            slot_grad = bag_sum(g_values, g_ids, group_lengths[:, 0], GROUPS * CAP)
            summed = summed + bag_sum(s_values, s_ids, group_lengths[:, 1], SMALL_ROWS)
            return (summed, slot_grad)
        small_grad, slot_grad = lax.scan(per_group, jnp.zeros((SMALL_ROWS, D), jnp.float32), (giant_values, small_values, slot_ids, length_table, small_table_ids))
        slot_grad = slot_grad.reshape(GROUPS, GROUPS, CAP, D)

        def per_owner(unused, owner_inputs):
            owner_blocks, owner_rows = owner_inputs
            empty = jnp.zeros((G_DEV, D), jnp.float32)
            return (unused, empty.at[owner_rows.reshape(-1)].add(owner_blocks.reshape(-1, D), mode='drop'))
        _, giant_grad = lax.scan(per_owner, jnp.float32(0.0), (jnp.transpose(slot_grad, (1, 0, 2, 3)), jnp.transpose(row_lists, (1, 0, 2))))
        giant_grad = giant_grad.reshape(GROUPS * G_DEV, D)
        new_gw, new_ga = rowwise_adagrad(g_weight, g_accum, giant_grad)
        new_sw, new_sa = rowwise_adagrad(s_weight, s_accum, small_grad)
        return (state, (new_gw, new_ga, new_sw, new_sa))
    table_inputs = (jnp.arange(N_COL, dtype=jnp.int32), giant_slot, touched_rows, bag_lengths, small_ids, giant_weight, giant_accum, small_weight, small_accum)
    _, results = lax.scan(per_table, jnp.float32(0.0), table_inputs)
    return (results[0], results[1], results[2], results[3])
```

```python
import functools

import jax
import jax.numpy as jnp
from jax import lax
from jax.experimental import pallas as pl
from jax.experimental.pallas import tpu as pltpu
from jax.sharding import PartitionSpec as P

LEARN = 0.5
TINY = 1e-08
BF = jnp.bfloat16
F32 = jnp.float32
VMEM_LIMIT = 48 * 1024 * 1024
TAG_ROWS = 16


def masked_ids(ids, lengths):
    live = lax.broadcasted_iota(jnp.int32, ids.shape, 1) < lengths[:, None]
    return jnp.where(live, ids, -1).T


def counts_kernel(ids_ref, out_ref):
    rows, samples = out_ref.shape
    bag = ids_ref.shape[0]
    lanes = 256
    first = pl.program_id(0) * rows
    local = lax.broadcasted_iota(jnp.int32, (16, lanes), 0)

    @pl.loop(0, samples // lanes)
    def _(chunk):
        at = pl.ds(pl.multiple_of(chunk * lanes, lanes), lanes)
        named = [jnp.broadcast_to(ids_ref[k : k + 1, at], (16, lanes)) for k in range(bag)]

        @pl.loop(0, rows // 16)
        def _(step):
            bucket = local + (first + step * 16)
            total = jnp.zeros((16, lanes), F32)
            for k in range(bag):
                total = total + jnp.where(named[k] == bucket, 1.0, 0.0)
            out_ref[pl.ds(pl.multiple_of(step * 16, 16), 16), at] = total.astype(BF)


def bag_counts(ids, buckets):
    bag, samples = ids.shape
    rows = 256
    return pl.pallas_call(
        counts_kernel,
        grid=(buckets // rows,),
        in_specs=[pl.BlockSpec((bag, samples), lambda i: (0, 0))],
        out_specs=pl.BlockSpec((rows, samples), lambda i: (i, 0)),
        out_shape=jax.ShapeDtypeStruct((buckets, samples), BF),
        compiler_params=pltpu.CompilerParams(vmem_limit_bytes=VMEM_LIMIT),
        cost_estimate=pl.CostEstimate(
            flops=3 * bag * buckets * samples, bytes_accessed=2 * buckets * samples, transcendentals=0
        ),
    )(ids)


def corner(array):
    lead = (1,) * (array.ndim - 2)
    return pl.BlockSpec(lead + (16, 128), lambda *_: (0,) * array.ndim)


def matmul_kernel(counts_ref, values_ref, left_ref, right_ref):
    sums = jnp.dot(counts_ref[...], values_ref[...], preferred_element_type=F32)
    half = left_ref.shape[1]
    left_ref[...] = sums[:, :half]
    right_ref[...] = sums[:, half:]


def packed_kernel(capacity, counts_ref, values_ref, later_ref, out_ref):
    del later_ref
    sums = jnp.dot(counts_ref[...], values_ref[...], preferred_element_type=F32)
    rows, width = sums.shape
    lanes = out_ref.shape[2]
    parts = width // lanes
    largest = jnp.maximum(jnp.max(jnp.abs(sums), axis=1, keepdims=True), 2.0**-100)
    power = jnp.floor(jnp.log2(largest) + 1e-3) - 14.0
    coded = jnp.round(sums * jnp.exp2(-power))
    coded = jnp.clip(coded, -32767.0, 32767.0).astype(jnp.int32).astype(jnp.int16)
    power = jnp.broadcast_to(power, (rows, lanes))
    for block in range(rows // capacity):
        mine = slice(block * capacity, (block + 1) * capacity)
        for part in range(parts):
            out_ref[block, part * capacity : (part + 1) * capacity, :] = coded[
                mine, part * lanes : (part + 1) * lanes
            ]
        tag = jnp.concatenate([power[mine, :], jnp.zeros((lanes - capacity, lanes), F32)], axis=0)
        out_ref[block, parts * capacity :, :] = tag.T[0:TAG_ROWS, :].astype(jnp.int32).astype(jnp.int16)


def bucket_sums(counts, values):
    buckets, samples = counts.shape
    width = values.shape[1]
    rows = 512
    return pl.pallas_call(
        matmul_kernel,
        grid=(buckets // rows,),
        in_specs=[
            pl.BlockSpec((rows, samples), lambda i: (i, 0)),
            pl.BlockSpec((samples, width), lambda i: (0, 0)),
        ],
        out_specs=[pl.BlockSpec((rows, width // 2), lambda i: (i, 0))] * 2,
        out_shape=[jax.ShapeDtypeStruct((buckets, width // 2), F32)] * 2,
        compiler_params=pltpu.CompilerParams(vmem_limit_bytes=VMEM_LIMIT),
    )(counts, values)


def packed_bucket_sums(counts, values, capacity, later):
    buckets, samples = counts.shape
    width = values.shape[1]
    rows, lanes = 512, 128
    tall = capacity * width // lanes + TAG_ROWS
    return pl.pallas_call(
        functools.partial(packed_kernel, capacity),
        grid=(buckets // rows,),
        in_specs=[
            pl.BlockSpec((rows, samples), lambda i: (i, 0)),
            pl.BlockSpec((samples, width), lambda i: (0, 0)),
            corner(later),
        ],
        out_specs=pl.BlockSpec((rows // capacity, tall, lanes), lambda i: (i, 0, 0)),
        out_shape=jax.ShapeDtypeStruct((buckets // capacity, tall, lanes), jnp.int16),
        compiler_params=pltpu.CompilerParams(vmem_limit_bytes=VMEM_LIMIT),
    )(counts, values, later)


def adagrad_step(weight_ref, accum_ref, grad, new_weight_ref, new_accum_ref):
    rows, width = grad.shape
    accum = jnp.broadcast_to(accum_ref[...], (8, rows)).T[:, 0:1]
    total = accum + jnp.sum(grad * grad, axis=1, keepdims=True) * (1.0 / width)
    new_weight_ref[...] = weight_ref[...] - grad * (LEARN / (jnp.sqrt(total) + TINY))
    new_accum_ref[...] = jnp.broadcast_to(total, (rows, 128)).T[0:1, :]


def giant_kernel(capacity, targets_ref, arrived_ref, weight_ref, accum_ref, new_weight_ref, new_accum_ref, parts):
    rows, width = weight_ref.shape
    groups, tall, lanes = arrived_ref.shape

    @pl.when(pl.program_id(0) == 0)
    def _():
        for group in range(groups):
            here = slice(group * capacity, (group + 1) * capacity)
            tag = arrived_ref[group, tall - TAG_ROWS :, :].astype(jnp.int32).astype(F32)
            scale = jnp.exp2(tag.T[0:capacity, 0:1])
            for part in range(width // lanes):
                value = arrived_ref[group, part * capacity : (part + 1) * capacity, :]
                value = value.astype(jnp.int32).astype(F32) * scale
                high = value.astype(BF)
                rest = value - high.astype(F32)
                middle = rest.astype(BF)
                low = (rest - middle.astype(F32)).astype(BF)
                for place, piece in enumerate((high, middle, low)):
                    at = place * width + part * lanes
                    parts[here, at : at + lanes] = piece

    sources = groups * capacity
    row = lax.broadcasted_iota(jnp.int32, (rows, sources), 0) + pl.program_id(0) * rows
    hit = jnp.where(jnp.broadcast_to(targets_ref[...], (rows, sources)) == row, 1.0, 0.0).astype(BF)
    product = jnp.dot(hit, parts[...], preferred_element_type=F32)
    grad = product[:, 0:width] + (product[:, width : 2 * width] + product[:, 2 * width :])
    adagrad_step(weight_ref, accum_ref, grad, new_weight_ref, new_accum_ref)


def giant_update(targets, arrived, weight, accum, capacity):
    total, width = weight.shape
    sources = targets.shape[1]
    rows = 256
    return pl.pallas_call(
        functools.partial(giant_kernel, capacity),
        grid=(total // rows,),
        in_specs=[
            pl.BlockSpec((1, sources), lambda i: (0, 0)),
            pl.BlockSpec(arrived.shape, lambda i: (0, 0, 0)),
            pl.BlockSpec((rows, width), lambda i: (i, 0)),
            pl.BlockSpec((1, rows), lambda i: (0, i)),
        ],
        out_specs=[
            pl.BlockSpec((rows, width), lambda i: (i, 0)),
            pl.BlockSpec((1, rows), lambda i: (0, i)),
        ],
        out_shape=[
            jax.ShapeDtypeStruct((total, width), F32),
            jax.ShapeDtypeStruct((1, total), F32),
        ],
        scratch_shapes=[pltpu.VMEM((sources, 3 * width), BF)],
        compiler_params=pltpu.CompilerParams(vmem_limit_bytes=VMEM_LIMIT),
    )(targets, arrived, weight, accum)


def small_kernel(left_ref, right_ref, weight_ref, accum_ref, new_weight_ref, new_accum_ref):
    grad = jnp.concatenate([left_ref[...], right_ref[...]], axis=1)
    adagrad_step(weight_ref, accum_ref, grad, new_weight_ref, new_accum_ref)


def small_update(left, right, weight, accum):
    total, width = weight.shape
    rows = 512
    half = pl.BlockSpec((rows, width // 2), lambda i: (i, 0))
    block = pl.BlockSpec((rows, width), lambda i: (i, 0))
    line = pl.BlockSpec((1, rows), lambda i: (0, i))
    return pl.pallas_call(
        small_kernel,
        grid=(total // rows,),
        in_specs=[half, half, block, line],
        out_specs=[block, line],
        out_shape=[
            jax.ShapeDtypeStruct((total, width), F32),
            jax.ShapeDtypeStruct((1, total), F32),
        ],
        compiler_params=pltpu.CompilerParams(vmem_limit_bytes=VMEM_LIMIT),
    )(left, right, weight, accum)


def after_kernel(*refs):
    del refs


def after(value, *others):
    place = pl.BlockSpec(memory_space=pl.ANY)
    return pl.pallas_call(
        after_kernel,
        grid=(1,),
        in_specs=[place] + [corner(other) for other in others],
        out_specs=place,
        out_shape=jax.ShapeDtypeStruct(value.shape, value.dtype),
        input_output_aliases={0: 0},
    )(value, *others)


def ring_sum(value, axis):
    size = lax.axis_size(axis)
    terms = [value]
    for step in range(1, size):
        terms.append(lax.ppermute(value, axis, [(i, (i + step) % size) for i in range(size)]))
    while len(terms) > 1:
        half = len(terms) // 2
        terms = [terms[i] + terms[i + half] for i in range(half)]
    return terms[0]


def body(
    pooled_grad,
    giant_slot,
    touched_rows,
    bag_lengths,
    small_ids,
    giant_weight,
    giant_accum,
    small_weight,
    small_accum,
):
    groups = lax.axis_size("row") * lax.axis_size("rep")
    owners = lax.axis_size("col")
    capacity = touched_rows.shape[3]
    width = small_weight.shape[2]
    samples = giant_slot.shape[2]
    exchange = functools.partial(lax.all_to_all, split_axis=0, concat_axis=0, tiled=True)

    pairs = pooled_grad[0].reshape(-1, owners, 2, width)
    small_values = exchange(pairs[:, :, 1, :].transpose(1, 0, 2), "col")
    lengths = bag_lengths[0, 0]
    small_counts = bag_counts(masked_ids(small_ids[0, 0], lengths[:, 1]), small_weight.shape[1])
    giant_counts = bag_counts(masked_ids(giant_slot[0, 0], lengths[:, 0]), groups * capacity)
    giant_out = after(pairs[:, :, 0, :].transpose(1, 0, 2), small_values, small_counts, giant_counts)
    giant_values = exchange(giant_out, "col").reshape(samples, width)

    left, right = bucket_sums(small_counts, small_values.reshape(samples, width))
    left = lax.psum_scatter(left, "rep", scatter_dimension=0, tiled=True)
    right = lax.psum_scatter(right, "rep", scatter_dimension=0, tiled=True)
    both = ring_sum(jnp.concatenate([left, right], axis=1), "row")
    left = lax.all_gather(both[:, : width // 2], "rep", axis=0, tiled=True)
    right = lax.all_gather(both[:, width // 2 :], "rep", axis=0, tiled=True)

    coded = packed_bucket_sums(giant_counts, giant_values, capacity, both)
    arrived = exchange(coded, ("row", "rep"))
    targets = touched_rows[0, :, 0, :].reshape(1, -1)
    new_gw, new_ga = giant_update(targets, arrived, giant_weight[0], giant_accum, capacity)
    new_sw, new_sa = small_update(left, right, small_weight[0], small_accum)
    return (new_gw[None], new_ga, new_sw[None], new_sa)


def solution(mesh):
    placed = (
        P(("row", "rep"), "col", None, None),
        P("col", ("row", "rep"), None, None),
        P("col", None, ("row", "rep"), None),
        P("col", ("row", "rep"), None, None),
        P("col", ("row", "rep"), None, None),
        P("col", ("row", "rep"), None),
        P("col", ("row", "rep")),
        P("col", None, None),
        P("col", None),
    )
    return jax.shard_map(
        body,
        mesh=mesh,
        in_specs=placed,
        out_specs=(
            P("col", ("row", "rep"), None),
            P("col", ("row", "rep")),
            P("col", None, None),
            P("col", None),
        ),
        check_vma=False,
    )
```

```python
import functools

import jax
import jax.numpy as jnp
from jax import lax
from jax.experimental import pallas as pl
from jax.experimental.pallas import tpu as pltpu
from jax.sharding import PartitionSpec as P

LEARN = 0.5
TINY = 1e-08
BF = jnp.bfloat16
F32 = jnp.float32
VMEM_LIMIT = 20 * 1024 * 1024
TAG_ROWS = 16


def masked_ids(ids, lengths):
    live = lax.broadcasted_iota(jnp.int32, ids.shape, 1) < lengths[:, None]
    return jnp.where(live, ids, -1).T


def counts_kernel(ids_ref, out_ref):
    rows, samples = out_ref.shape
    bag = ids_ref.shape[0]
    lanes = 256
    first = pl.program_id(0) * rows
    local = lax.broadcasted_iota(jnp.int32, (16, lanes), 0)

    @pl.loop(0, samples // lanes)
    def _(chunk):
        at = pl.ds(pl.multiple_of(chunk * lanes, lanes), lanes)
        named = [jnp.broadcast_to(ids_ref[k : k + 1, at], (16, lanes)) for k in range(bag)]

        @pl.loop(0, rows // 16)
        def _(step):
            bucket = local + (first + step * 16)
            total = jnp.zeros((16, lanes), F32)
            for k in range(bag):
                total = total + jnp.where(named[k] == bucket, 1.0, 0.0)
            out_ref[pl.ds(pl.multiple_of(step * 16, 16), 16), at] = total.astype(BF)


def bag_counts(ids, buckets):
    bag, samples = ids.shape
    rows = 256
    return pl.pallas_call(
        counts_kernel,
        grid=(buckets // rows,),
        in_specs=[pl.BlockSpec((bag, samples), lambda i: (0, 0))],
        out_specs=pl.BlockSpec((rows, samples), lambda i: (i, 0)),
        out_shape=jax.ShapeDtypeStruct((buckets, samples), BF),
        compiler_params=pltpu.CompilerParams(vmem_limit_bytes=VMEM_LIMIT),
        cost_estimate=pl.CostEstimate(
            flops=3 * bag * buckets * samples, bytes_accessed=2 * buckets * samples, transcendentals=0
        ),
    )(ids)


def corner(array):
    lead = (1,) * (array.ndim - 2)
    return pl.BlockSpec(lead + (16, 128), lambda *_: (0,) * array.ndim)


def matmul_kernel(counts_ref, values_ref, out_ref):
    out_ref[...] = jnp.dot(counts_ref[...], values_ref[...], preferred_element_type=F32)


def coded_rows(sums):
    largest = jnp.maximum(jnp.max(jnp.abs(sums), axis=1, keepdims=True), 2.0**-100)
    power = jnp.floor(jnp.log2(largest) + 1e-3) - 14.0
    coded = jnp.clip(jnp.round(sums * jnp.exp2(-power)), -32767.0, 32767.0)
    return coded.astype(jnp.int32).astype(jnp.int16), power


def packed_kernel(capacity, place_ref, counts_ref, values_ref, *refs):
    terms, out_ref = refs[:-1], refs[-1]
    sums = jnp.dot(counts_ref[...], values_ref[...], preferred_element_type=F32)
    coded, power = coded_rows(sums)
    rows, width = sums.shape
    lanes = out_ref.shape[2]
    mine = terms[0].shape[0] // len(terms)
    at = pl.ds(pl.multiple_of(place_ref[0] * mine, mine), mine)
    small = terms[0][at, :]
    for term in terms[1:]:
        small = small + term[at, :]
    small_coded, small_power = coded_rows(small)
    tall = capacity + mine
    diagonal = lax.broadcasted_iota(jnp.int32, (tall, lanes), 0) == lax.broadcasted_iota(jnp.int32, (tall, lanes), 1)
    for block in range(rows // capacity):
        slots = slice(block * capacity, (block + 1) * capacity)
        first = 0
        for piece, count in ((coded[slots, :], capacity), (small_coded, mine)):
            for part in range(width // lanes):
                out_ref[block, first : first + count, :] = piece[:, part * lanes : (part + 1) * lanes]
                first += count
        powers = jnp.concatenate([power[slots, :], small_power], axis=0)
        spread = jnp.where(diagonal, jnp.broadcast_to(powers, (tall, lanes)), 0.0)
        tag = jnp.broadcast_to(jnp.sum(spread, axis=0, keepdims=True), (TAG_ROWS, lanes))
        out_ref[block, first:, :] = tag.astype(jnp.int32).astype(jnp.int16)


def bucket_sums(counts, values):
    buckets, samples = counts.shape
    width = values.shape[1]
    rows = 512
    return pl.pallas_call(
        matmul_kernel,
        grid=(buckets // rows,),
        in_specs=[
            pl.BlockSpec((rows, samples), lambda i: (i, 0)),
            pl.BlockSpec((samples, width), lambda i: (0, 0)),
        ],
        out_specs=pl.BlockSpec((rows, width), lambda i: (i, 0)),
        out_shape=jax.ShapeDtypeStruct((buckets, width), F32),
        compiler_params=pltpu.CompilerParams(vmem_limit_bytes=VMEM_LIMIT),
    )(counts, values)


def packed_bucket_sums(counts, values, capacity, place, terms):
    buckets, samples = counts.shape
    width = values.shape[1]
    rows, lanes = 512, 128
    mine = terms[0].shape[0] // len(terms)
    tall = (capacity + mine) * width // lanes + TAG_ROWS
    whole = pl.BlockSpec(terms[0].shape, lambda i: (0, 0))
    return pl.pallas_call(
        functools.partial(packed_kernel, capacity),
        grid=(buckets // rows,),
        in_specs=[
            pl.BlockSpec(memory_space=pltpu.SMEM),
            pl.BlockSpec((rows, samples), lambda i: (i, 0)),
            pl.BlockSpec((samples, width), lambda i: (0, 0)),
        ]
        + [whole] * len(terms),
        out_specs=pl.BlockSpec((rows // capacity, tall, lanes), lambda i: (i, 0, 0)),
        out_shape=jax.ShapeDtypeStruct((buckets // capacity, tall, lanes), jnp.int16),
        compiler_params=pltpu.CompilerParams(vmem_limit_bytes=VMEM_LIMIT),
    )(place, counts, values, *terms)


def adagrad_step(weight, accum, grad):
    rows, width = grad.shape
    column = jnp.broadcast_to(accum, (8, rows)).T[:, 0:1]
    total = column + jnp.sum(grad * grad, axis=1, keepdims=True) * (1.0 / width)
    new_weight = weight - grad * (LEARN / (jnp.sqrt(total) + TINY))
    return new_weight, jnp.broadcast_to(total, (rows, 128)).T[0:1, :]


def decoded(coded, scale):
    return coded.astype(jnp.int32).astype(F32) * scale


def update_kernel(
    capacity,
    outer,
    targets_ref,
    arrived_ref,
    giant_weight_ref,
    giant_accum_ref,
    small_weight_ref,
    small_accum_ref,
    new_giant_weight_ref,
    new_giant_accum_ref,
    new_small_weight_ref,
    new_small_accum_ref,
    parts,
):
    rows, width = giant_weight_ref.shape
    groups, tall, lanes = arrived_ref.shape
    halves = width // lanes
    mine = (tall - TAG_ROWS) // halves - capacity

    def scales(group):
        tag = arrived_ref[group, tall - TAG_ROWS :, :].astype(jnp.int32).astype(F32)
        return jnp.exp2(tag.T[:, 0:1])

    @pl.when(pl.program_id(0) == 0)
    def _():
        for group in range(groups):
            here = slice(group * capacity, (group + 1) * capacity)
            scale = scales(group)[0:capacity]
            for part in range(halves):
                value = decoded(arrived_ref[group, part * capacity : (part + 1) * capacity, :], scale)
                high = value.astype(BF)
                rest = value - high.astype(F32)
                middle = rest.astype(BF)
                low = (rest - middle.astype(F32)).astype(BF)
                for place, piece in enumerate((high, middle, low)):
                    at = place * width + part * lanes
                    parts[here, at : at + lanes] = piece

    sources = groups * capacity
    row = lax.broadcasted_iota(jnp.int32, (rows, sources), 0) + pl.program_id(0) * rows
    hit = jnp.where(jnp.broadcast_to(targets_ref[...], (rows, sources)) == row, 1.0, 0.0).astype(BF)
    product = jnp.dot(hit, parts[...], preferred_element_type=F32)
    grad = product[:, 0:width] + (product[:, width : 2 * width] + product[:, 2 * width :])
    new_weight, new_accum = adagrad_step(giant_weight_ref[...], giant_accum_ref[...], grad)
    new_giant_weight_ref[...] = new_weight
    new_giant_accum_ref[...] = new_accum

    band = outer * mine
    inner = groups // outer
    bands = small_weight_ref.shape[0] // band
    for local in range(bands):
        at = slice(local * band, (local + 1) * band)
        pieces = []
        for place in range(outer):
            group = place * inner + pl.program_id(0) * bands + local
            scale = scales(group)[capacity : capacity + mine]
            pair = []
            for part in range(halves):
                first = halves * capacity + part * mine
                pair.append(decoded(arrived_ref[group, first : first + mine, :], scale))
            pieces.append(jnp.concatenate(pair, axis=1))
        grad = jnp.concatenate(pieces, axis=0)
        new_weight, new_accum = adagrad_step(small_weight_ref[at, :], small_accum_ref[:, at], grad)
        new_small_weight_ref[at, :] = new_weight
        new_small_accum_ref[:, at] = new_accum


def update(targets, arrived, giant_weight, giant_accum, small_weight, small_accum, capacity, outer):
    giant_rows, width = giant_weight.shape
    small_rows = small_weight.shape[0]
    sources = targets.shape[1]
    steps = 4

    def blocks(rows):
        return [pl.BlockSpec((rows // steps, width), lambda i: (i, 0)), pl.BlockSpec((1, rows // steps), lambda i: (0, i))]

    def shapes(rows):
        return [jax.ShapeDtypeStruct((rows, width), F32), jax.ShapeDtypeStruct((1, rows), F32)]

    return pl.pallas_call(
        functools.partial(update_kernel, capacity, outer),
        grid=(steps,),
        in_specs=[
            pl.BlockSpec((1, sources), lambda i: (0, 0)),
            pl.BlockSpec(arrived.shape, lambda i: (0, 0, 0)),
        ]
        + blocks(giant_rows)
        + blocks(small_rows),
        out_specs=blocks(giant_rows) + blocks(small_rows),
        out_shape=shapes(giant_rows) + shapes(small_rows),
        scratch_shapes=[pltpu.VMEM((sources, 3 * width), BF)],
        compiler_params=pltpu.CompilerParams(vmem_limit_bytes=VMEM_LIMIT),
    )(targets, arrived, giant_weight, giant_accum, small_weight, small_accum)


def after_kernel(*refs):
    del refs


def after(value, *others):
    place = pl.BlockSpec(memory_space=pl.ANY)
    return pl.pallas_call(
        after_kernel,
        grid=(1,),
        in_specs=[place] + [corner(other) for other in others],
        out_specs=place,
        out_shape=jax.ShapeDtypeStruct(value.shape, value.dtype),
        input_output_aliases={0: 0},
    )(value, *others)


def ring_terms(value, axis):
    size = lax.axis_size(axis)
    terms = [value]
    for step in range(1, size):
        terms.append(lax.ppermute(value, axis, [(i, (i + step) % size) for i in range(size)]))
    return terms


def body(
    pooled_grad,
    giant_slot,
    touched_rows,
    bag_lengths,
    small_ids,
    giant_weight,
    giant_accum,
    small_weight,
    small_accum,
):
    groups = lax.axis_size("row") * lax.axis_size("rep")
    owners = lax.axis_size("col")
    capacity = touched_rows.shape[3]
    width = small_weight.shape[2]
    samples = giant_slot.shape[2]
    exchange = functools.partial(lax.all_to_all, split_axis=0, concat_axis=0, tiled=True)

    pairs = pooled_grad[0].reshape(-1, owners, 2, width)
    small_values = exchange(pairs[:, :, 1, :].transpose(1, 0, 2), "col")
    lengths = bag_lengths[0, 0]
    small_counts = bag_counts(masked_ids(small_ids[0, 0], lengths[:, 1]), small_weight.shape[1])
    giant_counts = bag_counts(masked_ids(giant_slot[0, 0], lengths[:, 0]), groups * capacity)
    small_sum = bucket_sums(small_counts, small_values.reshape(samples, width))

    giant_out = after(pairs[:, :, 0, :].transpose(1, 0, 2), small_sum, giant_counts)
    giant_values = exchange(giant_out, "col").reshape(samples, width)

    small_sum = lax.psum_scatter(small_sum, "rep", scatter_dimension=0, tiled=True)
    terms = ring_terms(small_sum, "row")
    place = lax.axis_index("row").astype(jnp.int32).reshape(1)

    packed = packed_bucket_sums(giant_counts, giant_values, capacity, place, terms)
    arrived = exchange(packed, ("row", "rep"))
    targets = touched_rows[0, :, 0, :].reshape(1, -1)
    new_gw, new_ga, new_sw, new_sa = update(
        targets, arrived, giant_weight[0], giant_accum, small_weight[0], small_accum, capacity, len(terms)
    )
    return (new_gw[None], new_ga, new_sw[None], new_sa)


def solution(mesh):
    placed = (
        P(("row", "rep"), "col", None, None),
        P("col", ("row", "rep"), None, None),
        P("col", None, ("row", "rep"), None),
        P("col", ("row", "rep"), None, None),
        P("col", ("row", "rep"), None, None),
        P("col", ("row", "rep"), None),
        P("col", ("row", "rep")),
        P("col", None, None),
        P("col", None),
    )
    return jax.shard_map(
        body,
        mesh=mesh,
        in_specs=placed,
        out_specs=(
            P("col", ("row", "rep"), None),
            P("col", ("row", "rep")),
            P("col", None, None),
            P("col", None),
        ),
        check_vma=False,
    )
```

```python
import functools

import jax
import jax.numpy as jnp
from jax import lax
from jax.experimental import pallas as pl
from jax.experimental.pallas import tpu as pltpu
from jax.sharding import PartitionSpec as P

LEARN = 0.5
TINY = 1e-08
BF = jnp.bfloat16
F32 = jnp.float32
VMEM_LIMIT = 48 * 1024 * 1024
TAG_ROWS = 16


def masked_ids(ids, lengths):
    live = lax.broadcasted_iota(jnp.int32, ids.shape, 1) < lengths[:, None]
    return jnp.where(live, ids, -1).T


def counts_kernel(ids_ref, out_ref):
    rows, samples = out_ref.shape
    bag = ids_ref.shape[0]
    lanes, tile = 256, 32
    first = pl.program_id(0) * rows
    local = lax.broadcasted_iota(jnp.int32, (tile, lanes), 0)

    @pl.loop(0, samples // lanes)
    def _(chunk):
        at = pl.ds(pl.multiple_of(chunk * lanes, lanes), lanes)
        named = [jnp.broadcast_to(ids_ref[k : k + 1, at], (tile, lanes)) for k in range(bag)]

        @pl.loop(0, rows // tile)
        def _(step):
            bucket = local + (first + step * tile)
            total = jnp.zeros((tile, lanes), jnp.int32)
            for k in range(bag):
                total = total + jnp.where(named[k] == bucket, 1, 0)
            out_ref[pl.ds(pl.multiple_of(step * tile, tile), tile), at] = total.astype(jnp.int8)


def bag_counts(ids, buckets):
    bag, samples = ids.shape
    rows = 256
    return pl.pallas_call(
        counts_kernel,
        grid=(buckets // rows,),
        in_specs=[pl.BlockSpec((bag, samples), lambda i: (0, 0))],
        out_specs=pl.BlockSpec((rows, samples), lambda i: (i, 0)),
        out_shape=jax.ShapeDtypeStruct((buckets, samples), jnp.int8),
        compiler_params=pltpu.CompilerParams(vmem_limit_bytes=VMEM_LIMIT),
        cost_estimate=pl.CostEstimate(
            flops=3 * bag * buckets * samples, bytes_accessed=buckets * samples, transcendentals=0
        ),
    )(ids)


def corner(array):
    lead = (1,) * (array.ndim - 2)
    return pl.BlockSpec(lead + (32, 128), lambda *_: (0,) * array.ndim)


def split_kernel(place_ref, counts_ref, values_ref, *refs):
    outs, sums = refs[:-1], refs[-1]
    rows = counts_ref.shape[0]
    at = pl.ds(pl.multiple_of(pl.program_id(0) * rows, rows), rows)
    sums[at, :] = jnp.dot(counts_ref[...].astype(BF), values_ref[...], preferred_element_type=F32)

    @pl.when(pl.program_id(0) == pl.num_programs(0) - 1)
    def _():
        piece = outs[0].shape[0]
        for step, out_ref in enumerate(outs):
            member = lax.rem(place_ref[0] + step, len(outs))
            out_ref[...] = sums[pl.ds(pl.multiple_of(member * piece, piece), piece), :]


def coded_rows(sums):
    largest = jnp.maximum(jnp.max(jnp.abs(sums), axis=1, keepdims=True), 2.0**-100)
    power = jnp.floor(jnp.log2(largest) + 1e-3) - 14.0
    coded = jnp.clip(jnp.round(sums * jnp.exp2(-power)), -32767.0, 32767.0)
    return coded.astype(jnp.int32).astype(jnp.int16), power


def packed_kernel(capacity, place_ref, counts_ref, values_ref, *refs):
    terms, out_ref = refs[:-1], refs[-1]
    sums = jnp.dot(counts_ref[...].astype(BF), values_ref[...], preferred_element_type=F32)
    coded, power = coded_rows(sums)
    rows, width = sums.shape
    lanes = out_ref.shape[2]
    mine = terms[0].shape[0] // len(terms)
    at = pl.ds(pl.multiple_of(place_ref[0] * mine, mine), mine)
    small = terms[0][at, :]
    for term in terms[1:]:
        small = small + term[at, :]
    small_coded, small_power = coded_rows(small)
    tall = capacity + mine
    diagonal = lax.broadcasted_iota(jnp.int32, (tall, lanes), 0) == lax.broadcasted_iota(jnp.int32, (tall, lanes), 1)
    for block in range(rows // capacity):
        slots = slice(block * capacity, (block + 1) * capacity)
        first = 0
        for piece, count in ((coded[slots, :], capacity), (small_coded, mine)):
            for part in range(width // lanes):
                out_ref[block, first : first + count, :] = piece[:, part * lanes : (part + 1) * lanes]
                first += count
        powers = jnp.concatenate([power[slots, :], small_power], axis=0)
        spread = jnp.where(diagonal, jnp.broadcast_to(powers, (tall, lanes)), 0.0)
        tag = jnp.broadcast_to(jnp.sum(spread, axis=0, keepdims=True), (TAG_ROWS, lanes))
        out_ref[block, first:, :] = tag.astype(jnp.int32).astype(jnp.int16)


def split_bucket_sums(counts, values, place, members):
    buckets, samples = counts.shape
    width = values.shape[1]
    rows = 512
    piece = (buckets // members, width)
    return pl.pallas_call(
        split_kernel,
        grid=(buckets // rows,),
        in_specs=[
            pl.BlockSpec(memory_space=pltpu.SMEM),
            pl.BlockSpec((rows, samples), lambda i: (i, 0)),
            pl.BlockSpec((samples, width), lambda i: (0, 0)),
        ],
        out_specs=[pl.BlockSpec(piece, lambda i: (0, 0))] * members,
        out_shape=[jax.ShapeDtypeStruct(piece, F32)] * members,
        scratch_shapes=[pltpu.VMEM((buckets, width), F32)],
        compiler_params=pltpu.CompilerParams(vmem_limit_bytes=VMEM_LIMIT),
    )(place, counts, values)


def packed_bucket_sums(counts, values, capacity, place, terms):
    buckets, samples = counts.shape
    width = values.shape[1]
    rows, lanes = 1024, 128
    mine = terms[0].shape[0] // len(terms)
    tall = (capacity + mine) * width // lanes + TAG_ROWS
    whole = pl.BlockSpec(terms[0].shape, lambda i: (0, 0))
    return pl.pallas_call(
        functools.partial(packed_kernel, capacity),
        grid=(buckets // rows,),
        in_specs=[
            pl.BlockSpec(memory_space=pltpu.SMEM),
            pl.BlockSpec((rows, samples), lambda i: (i, 0)),
            pl.BlockSpec((samples, width), lambda i: (0, 0)),
        ]
        + [whole] * len(terms),
        out_specs=pl.BlockSpec((rows // capacity, tall, lanes), lambda i: (i, 0, 0)),
        out_shape=jax.ShapeDtypeStruct((buckets // capacity, tall, lanes), jnp.int16),
        compiler_params=pltpu.CompilerParams(vmem_limit_bytes=VMEM_LIMIT),
    )(place, counts, values, *terms)


def adagrad_step(weight, accum, grad):
    rows, width = grad.shape
    column = jnp.broadcast_to(accum, (8, rows)).T[:, 0:1]
    total = column + jnp.sum(grad * grad, axis=1, keepdims=True) * (1.0 / width)
    new_weight = weight - grad * (LEARN / (jnp.sqrt(total) + TINY))
    return new_weight, jnp.broadcast_to(total, (rows, 128)).T[0:1, :]


def decoded(coded, scale):
    return coded.astype(jnp.int32).astype(F32) * scale


def update_kernel(
    capacity,
    outer,
    targets_ref,
    arrived_ref,
    giant_weight_ref,
    giant_accum_ref,
    small_weight_ref,
    small_accum_ref,
    new_giant_weight_ref,
    new_giant_accum_ref,
    new_small_weight_ref,
    new_small_accum_ref,
    parts,
):
    rows, width = giant_weight_ref.shape
    groups, tall, lanes = arrived_ref.shape
    halves = width // lanes
    mine = (tall - TAG_ROWS) // halves - capacity

    def scales(group):
        tag = arrived_ref[group, tall - TAG_ROWS :, :].astype(jnp.int32).astype(F32)
        return jnp.exp2(tag.T[:, 0:1])

    @pl.when(pl.program_id(0) == 0)
    def _():
        for group in range(groups):
            here = slice(group * capacity, (group + 1) * capacity)
            scale = scales(group)[0:capacity]
            for part in range(halves):
                value = decoded(arrived_ref[group, part * capacity : (part + 1) * capacity, :], scale)
                high = value.astype(BF)
                rest = value - high.astype(F32)
                middle = rest.astype(BF)
                low = (rest - middle.astype(F32)).astype(BF)
                for place, piece in enumerate((high, middle, low)):
                    at = place * width + part * lanes
                    parts[here, at : at + lanes] = piece

    sources = groups * capacity
    row = lax.broadcasted_iota(jnp.int32, (rows, sources), 0) + pl.program_id(0) * rows
    hit = jnp.where(jnp.broadcast_to(targets_ref[...], (rows, sources)) == row, 1.0, 0.0).astype(BF)
    product = jnp.dot(hit, parts[...], preferred_element_type=F32)
    grad = product[:, 0:width] + (product[:, width : 2 * width] + product[:, 2 * width :])
    new_weight, new_accum = adagrad_step(giant_weight_ref[...], giant_accum_ref[...], grad)
    new_giant_weight_ref[...] = new_weight
    new_giant_accum_ref[...] = new_accum

    band = outer * mine
    inner = groups // outer
    bands = small_weight_ref.shape[0] // band
    for local in range(bands):
        at = slice(local * band, (local + 1) * band)
        pieces = []
        for place in range(outer):
            group = place * inner + pl.program_id(0) * bands + local
            scale = scales(group)[capacity : capacity + mine]
            pair = []
            for part in range(halves):
                first = halves * capacity + part * mine
                pair.append(decoded(arrived_ref[group, first : first + mine, :], scale))
            pieces.append(jnp.concatenate(pair, axis=1))
        grad = jnp.concatenate(pieces, axis=0)
        new_weight, new_accum = adagrad_step(small_weight_ref[at, :], small_accum_ref[:, at], grad)
        new_small_weight_ref[at, :] = new_weight
        new_small_accum_ref[:, at] = new_accum


def update(targets, arrived, giant_weight, giant_accum, small_weight, small_accum, capacity, outer):
    giant_rows, width = giant_weight.shape
    small_rows = small_weight.shape[0]
    sources = targets.shape[1]
    steps = 4

    def blocks(rows):
        return [pl.BlockSpec((rows // steps, width), lambda i: (i, 0)), pl.BlockSpec((1, rows // steps), lambda i: (0, i))]

    def shapes(rows):
        return [jax.ShapeDtypeStruct((rows, width), F32), jax.ShapeDtypeStruct((1, rows), F32)]

    return pl.pallas_call(
        functools.partial(update_kernel, capacity, outer),
        grid=(steps,),
        in_specs=[
            pl.BlockSpec((1, sources), lambda i: (0, 0)),
            pl.BlockSpec(arrived.shape, lambda i: (0, 0, 0)),
        ]
        + blocks(giant_rows)
        + blocks(small_rows),
        out_specs=blocks(giant_rows) + blocks(small_rows),
        out_shape=shapes(giant_rows) + shapes(small_rows),
        scratch_shapes=[pltpu.VMEM((sources, 3 * width), BF)],
        compiler_params=pltpu.CompilerParams(vmem_limit_bytes=VMEM_LIMIT),
    )(targets, arrived, giant_weight, giant_accum, small_weight, small_accum)


def after_kernel(*refs):
    del refs


def after(value, *others):
    place = pl.BlockSpec(memory_space=pl.ANY)
    return pl.pallas_call(
        after_kernel,
        grid=(1,),
        in_specs=[place] + [corner(other) for other in others],
        out_specs=place,
        out_shape=jax.ShapeDtypeStruct(value.shape, value.dtype),
        input_output_aliases={0: 0},
    )(value, *others)


def moved(value, axis, step):
    size = lax.axis_size(axis)
    return lax.ppermute(value, axis, [(i, (i + step) % size) for i in range(size)])


def position(axis):
    return lax.axis_index(axis).astype(jnp.int32).reshape(1)


def body(
    pooled_grad,
    giant_slot,
    touched_rows,
    bag_lengths,
    small_ids,
    giant_weight,
    giant_accum,
    small_weight,
    small_accum,
):
    groups = lax.axis_size("row") * lax.axis_size("rep")
    owners = lax.axis_size("col")
    capacity = touched_rows.shape[3]
    width = small_weight.shape[2]
    samples = giant_slot.shape[2]
    exchange = functools.partial(lax.all_to_all, split_axis=0, concat_axis=0, tiled=True)

    pairs = pooled_grad[0].reshape(-1, owners, 2, width)
    small_values = exchange(pairs[:, :, 1, :].transpose(1, 0, 2), "col")
    lengths = bag_lengths[0, 0]
    small_counts = bag_counts(masked_ids(small_ids[0, 0], lengths[:, 1]), small_weight.shape[1])
    giant_counts = bag_counts(masked_ids(giant_slot[0, 0], lengths[:, 0]), groups * capacity)
    giant_out = after(pairs[:, :, 0, :].transpose(1, 0, 2), small_values, small_counts, giant_counts)
    giant_values = exchange(giant_out, "col").reshape(samples, width)

    pieces = split_bucket_sums(small_counts, small_values.reshape(samples, width), position("rep"), lax.axis_size("rep"))
    small_sum = sum(moved(piece, "rep", step) if step else piece for step, piece in enumerate(pieces))
    terms = [moved(small_sum, "row", step) if step else small_sum for step in range(lax.axis_size("row"))]

    packed = packed_bucket_sums(giant_counts, giant_values, capacity, position("row"), terms)
    arrived = exchange(packed, ("row", "rep"))
    targets = touched_rows[0, :, 0, :].reshape(1, -1)
    new_gw, new_ga, new_sw, new_sa = update(
        targets, arrived, giant_weight[0], giant_accum, small_weight[0], small_accum, capacity, len(terms)
    )
    return (new_gw[None], new_ga, new_sw[None], new_sa)


def solution(mesh):
    placed = (
        P(("row", "rep"), "col", None, None),
        P("col", ("row", "rep"), None, None),
        P("col", None, ("row", "rep"), None),
        P("col", ("row", "rep"), None, None),
        P("col", ("row", "rep"), None, None),
        P("col", ("row", "rep"), None),
        P("col", ("row", "rep")),
        P("col", None, None),
        P("col", None),
    )
    return jax.shard_map(
        body,
        mesh=mesh,
        in_specs=placed,
        out_specs=(
            P("col", ("row", "rep"), None),
            P("col", ("row", "rep")),
            P("col", None, None),
            P("col", None),
        ),
        check_vma=False,
    )
```

```python
import functools

import jax
import jax.numpy as jnp
from jax import lax
from jax.experimental import pallas as pl
from jax.experimental.pallas import tpu as pltpu
from jax.sharding import PartitionSpec as P

LEARN = 0.5
TINY = 1e-08
BF = jnp.bfloat16
F32 = jnp.float32
VMEM_LIMIT = 48 * 1024 * 1024
TAG_ROWS = 16


def masked_ids(ids, lengths):
    live = lax.broadcasted_iota(jnp.int32, ids.shape, 1) < lengths[:, None]
    return jnp.where(live, ids, -1).T


def counts_kernel(ids_ref, out_ref):
    rows, samples = out_ref.shape
    bag = ids_ref.shape[0]
    lanes, tile = 256, 32
    first = pl.program_id(0) * rows
    local = lax.broadcasted_iota(jnp.int32, (tile, lanes), 0)

    @pl.loop(0, samples // lanes)
    def _(chunk):
        at = pl.ds(pl.multiple_of(chunk * lanes, lanes), lanes)
        named = [jnp.broadcast_to(ids_ref[k : k + 1, at], (tile, lanes)) for k in range(bag)]

        @pl.loop(0, rows // tile)
        def _(step):
            bucket = local + (first + step * tile)
            total = jnp.zeros((tile, lanes), jnp.int32)
            for k in range(bag):
                total = total + jnp.where(named[k] == bucket, 1, 0)
            out_ref[pl.ds(pl.multiple_of(step * tile, tile), tile), at] = total.astype(jnp.int8)


def bag_counts(ids, buckets):
    bag, samples = ids.shape
    rows = 256
    return pl.pallas_call(
        counts_kernel,
        grid=(buckets // rows,),
        in_specs=[pl.BlockSpec((bag, samples), lambda i: (0, 0))],
        out_specs=pl.BlockSpec((rows, samples), lambda i: (i, 0)),
        out_shape=jax.ShapeDtypeStruct((buckets, samples), jnp.int8),
        compiler_params=pltpu.CompilerParams(vmem_limit_bytes=VMEM_LIMIT),
        cost_estimate=pl.CostEstimate(
            flops=3 * bag * buckets * samples, bytes_accessed=buckets * samples, transcendentals=0
        ),
    )(ids)


def corner(array):
    lead = (1,) * (array.ndim - 2)
    return pl.BlockSpec(lead + (32, 128), lambda *_: (0,) * array.ndim)


def cut(sums, place, outs):
    piece = outs[0].shape[0]
    for step, out_ref in enumerate(outs):
        member = lax.rem(place + step, len(outs))
        out_ref[...] = sums[pl.ds(pl.multiple_of(member * piece, piece), piece), :]


def split_kernel(place_ref, counts_ref, values_ref, *refs):
    outs, sums = refs[:-1], refs[-1]
    rows = counts_ref.shape[0]
    at = pl.ds(pl.multiple_of(pl.program_id(0) * rows, rows), rows)
    sums[at, :] = jnp.dot(counts_ref[...].astype(BF), values_ref[...], preferred_element_type=F32)

    @pl.when(pl.program_id(0) == pl.num_programs(0) - 1)
    def _():
        cut(sums, place_ref[0], outs)


def halves_kernel(count, distance, place_ref, *refs):
    terms, outs, sums = refs[:count], refs[count:-1], refs[-1]
    total = terms[0][...]
    for term in terms[1:]:
        total = total + term[...]
    sums[...] = total
    cut(sums, lax.div(place_ref[0], distance), outs)


def coded_rows(sums):
    largest = jnp.maximum(jnp.max(jnp.abs(sums), axis=1, keepdims=True), 2.0**-100)
    power = jnp.floor(jnp.log2(largest) + 1e-3) - 14.0
    coded = jnp.clip(jnp.round(sums * jnp.exp2(-power)), -32767.0, 32767.0)
    return coded.astype(jnp.int32).astype(jnp.int16), power


def packed_kernel(capacity, counts_ref, values_ref, *refs):
    terms, out_ref = refs[:-1], refs[-1]
    sums = jnp.dot(counts_ref[...].astype(BF), values_ref[...], preferred_element_type=F32)
    coded, power = coded_rows(sums)
    rows, width = sums.shape
    lanes = out_ref.shape[2]
    mine = terms[0].shape[0]
    small = terms[0][...]
    for term in terms[1:]:
        small = small + term[...]
    small_coded, small_power = coded_rows(small)
    tall = capacity + mine
    diagonal = lax.broadcasted_iota(jnp.int32, (tall, lanes), 0) == lax.broadcasted_iota(jnp.int32, (tall, lanes), 1)
    for block in range(rows // capacity):
        slots = slice(block * capacity, (block + 1) * capacity)
        first = 0
        for piece, count in ((coded[slots, :], capacity), (small_coded, mine)):
            for part in range(width // lanes):
                out_ref[block, first : first + count, :] = piece[:, part * lanes : (part + 1) * lanes]
                first += count
        powers = jnp.concatenate([power[slots, :], small_power], axis=0)
        spread = jnp.where(diagonal, jnp.broadcast_to(powers, (tall, lanes)), 0.0)
        tag = jnp.broadcast_to(jnp.sum(spread, axis=0, keepdims=True), (TAG_ROWS, lanes))
        out_ref[block, first:, :] = tag.astype(jnp.int32).astype(jnp.int16)


def split_bucket_sums(counts, values, place, members):
    buckets, samples = counts.shape
    width = values.shape[1]
    rows = 512
    piece = (buckets // members, width)
    return pl.pallas_call(
        split_kernel,
        grid=(buckets // rows,),
        in_specs=[
            pl.BlockSpec(memory_space=pltpu.SMEM),
            pl.BlockSpec((rows, samples), lambda i: (i, 0)),
            pl.BlockSpec((samples, width), lambda i: (0, 0)),
        ],
        out_specs=[pl.BlockSpec(piece, lambda i: (0, 0))] * members,
        out_shape=[jax.ShapeDtypeStruct(piece, F32)] * members,
        scratch_shapes=[pltpu.VMEM((buckets, width), F32)],
        compiler_params=pltpu.CompilerParams(vmem_limit_bytes=VMEM_LIMIT),
    )(place, counts, values)


def split_halves(terms, place, distance):
    rows, width = terms[0].shape
    piece = (rows // 2, width)
    return pl.pallas_call(
        functools.partial(halves_kernel, len(terms), distance),
        in_specs=[pl.BlockSpec(memory_space=pltpu.SMEM)] + [pl.BlockSpec(memory_space=pltpu.VMEM)] * len(terms),
        out_specs=[pl.BlockSpec(memory_space=pltpu.VMEM)] * 2,
        out_shape=[jax.ShapeDtypeStruct(piece, F32)] * 2,
        scratch_shapes=[pltpu.VMEM((rows, width), F32)],
        compiler_params=pltpu.CompilerParams(vmem_limit_bytes=VMEM_LIMIT),
    )(place, *terms)


def packed_bucket_sums(counts, values, capacity, terms):
    buckets, samples = counts.shape
    width = values.shape[1]
    rows, lanes = 512, 128
    mine = terms[0].shape[0]
    tall = (capacity + mine) * width // lanes + TAG_ROWS
    whole = pl.BlockSpec(terms[0].shape, lambda i: (0, 0))
    return pl.pallas_call(
        functools.partial(packed_kernel, capacity),
        grid=(buckets // rows,),
        in_specs=[
            pl.BlockSpec((rows, samples), lambda i: (i, 0)),
            pl.BlockSpec((samples, width), lambda i: (0, 0)),
        ]
        + [whole] * len(terms),
        out_specs=pl.BlockSpec((rows // capacity, tall, lanes), lambda i: (i, 0, 0)),
        out_shape=jax.ShapeDtypeStruct((buckets // capacity, tall, lanes), jnp.int16),
        compiler_params=pltpu.CompilerParams(vmem_limit_bytes=VMEM_LIMIT),
    )(counts, values, *terms)


def adagrad_step(weight, accum, grad):
    rows, width = grad.shape
    column = jnp.broadcast_to(accum, (8, rows)).T[:, 0:1]
    total = column + jnp.sum(grad * grad, axis=1, keepdims=True) * (1.0 / width)
    new_weight = weight - grad * (LEARN / (jnp.sqrt(total) + TINY))
    return new_weight, jnp.broadcast_to(total, (rows, 128)).T[0:1, :]


def decoded(coded, scale):
    return coded.astype(jnp.int32).astype(F32) * scale


def update_kernel(
    capacity,
    targets_ref,
    arrived_ref,
    giant_weight_ref,
    giant_accum_ref,
    small_weight_ref,
    small_accum_ref,
    new_giant_weight_ref,
    new_giant_accum_ref,
    new_small_weight_ref,
    new_small_accum_ref,
    parts,
):
    rows, width = giant_weight_ref.shape
    groups, tall, lanes = arrived_ref.shape
    halves = width // lanes
    mine = (tall - TAG_ROWS) // halves - capacity

    def scales(group):
        tag = arrived_ref[group, tall - TAG_ROWS :, :].astype(jnp.int32).astype(F32)
        return jnp.exp2(tag.T[:, 0:1])

    @pl.when(pl.program_id(0) == 0)
    def _():
        for group in range(groups):
            here = slice(group * capacity, (group + 1) * capacity)
            scale = scales(group)[0:capacity]
            for part in range(halves):
                value = decoded(arrived_ref[group, part * capacity : (part + 1) * capacity, :], scale)
                high = value.astype(BF)
                rest = value - high.astype(F32)
                middle = rest.astype(BF)
                low = (rest - middle.astype(F32)).astype(BF)
                for place, piece in enumerate((high, middle, low)):
                    at = place * width + part * lanes
                    parts[here, at : at + lanes] = piece

    sources = groups * capacity
    row = lax.broadcasted_iota(jnp.int32, (rows, sources), 0) + pl.program_id(0) * rows
    hit = jnp.where(jnp.broadcast_to(targets_ref[...], (rows, sources)) == row, 1.0, 0.0).astype(BF)
    product = jnp.dot(hit, parts[...], preferred_element_type=F32)
    grad = product[:, 0:width] + (product[:, width : 2 * width] + product[:, 2 * width :])
    new_weight, new_accum = adagrad_step(giant_weight_ref[...], giant_accum_ref[...], grad)
    new_giant_weight_ref[...] = new_weight
    new_giant_accum_ref[...] = new_accum

    band = lanes // mine
    local_groups = small_weight_ref.shape[0] // mine
    for local in range(0, local_groups, band):
        at = slice(local * mine, (local + band) * mine)
        pieces = []
        for place in range(band):
            group = pl.program_id(0) * local_groups + local + place
            scale = scales(group)[capacity : capacity + mine]
            pair = []
            for part in range(halves):
                first = halves * capacity + part * mine
                pair.append(decoded(arrived_ref[group, first : first + mine, :], scale))
            pieces.append(jnp.concatenate(pair, axis=1))
        grad = jnp.concatenate(pieces, axis=0)
        new_weight, new_accum = adagrad_step(small_weight_ref[at, :], small_accum_ref[:, at], grad)
        new_small_weight_ref[at, :] = new_weight
        new_small_accum_ref[:, at] = new_accum


def update(targets, arrived, giant_weight, giant_accum, small_weight, small_accum, capacity):
    giant_rows, width = giant_weight.shape
    small_rows = small_weight.shape[0]
    sources = targets.shape[1]
    steps = 2

    def blocks(rows):
        return [pl.BlockSpec((rows // steps, width), lambda i: (i, 0)), pl.BlockSpec((1, rows // steps), lambda i: (0, i))]

    def shapes(rows):
        return [jax.ShapeDtypeStruct((rows, width), F32), jax.ShapeDtypeStruct((1, rows), F32)]

    return pl.pallas_call(
        functools.partial(update_kernel, capacity),
        grid=(steps,),
        in_specs=[
            pl.BlockSpec((1, sources), lambda i: (0, 0)),
            pl.BlockSpec(arrived.shape, lambda i: (0, 0, 0)),
        ]
        + blocks(giant_rows)
        + blocks(small_rows),
        out_specs=blocks(giant_rows) + blocks(small_rows),
        out_shape=shapes(giant_rows) + shapes(small_rows),
        scratch_shapes=[pltpu.VMEM((sources, 3 * width), BF)],
        compiler_params=pltpu.CompilerParams(vmem_limit_bytes=VMEM_LIMIT),
    )(targets, arrived, giant_weight, giant_accum, small_weight, small_accum)


def after_kernel(*refs):
    del refs


def after(value, *others):
    place = pl.BlockSpec(memory_space=pl.ANY)
    return pl.pallas_call(
        after_kernel,
        grid=(1,),
        in_specs=[place] + [corner(other) for other in others],
        out_specs=place,
        out_shape=jax.ShapeDtypeStruct(value.shape, value.dtype),
        input_output_aliases={0: 0},
    )(value, *others)


def moved(value, axis, step):
    size = lax.axis_size(axis)
    return lax.ppermute(value, axis, [(i, (i + step) % size) for i in range(size)])


def position(axis):
    return lax.axis_index(axis).astype(jnp.int32).reshape(1)


def body(
    pooled_grad,
    giant_slot,
    touched_rows,
    bag_lengths,
    small_ids,
    giant_weight,
    giant_accum,
    small_weight,
    small_accum,
):
    groups = lax.axis_size("row") * lax.axis_size("rep")
    owners = lax.axis_size("col")
    capacity = touched_rows.shape[3]
    width = small_weight.shape[2]
    samples = giant_slot.shape[2]
    exchange = functools.partial(lax.all_to_all, split_axis=0, concat_axis=0, tiled=True)

    tables = pooled_grad[0].reshape(-1, owners, 2, width).transpose(1, 2, 0, 3)
    small_values = exchange(tables[:, 1], "col")
    lengths = bag_lengths[0, 0]
    small_counts = bag_counts(masked_ids(small_ids[0, 0], lengths[:, 1]), small_weight.shape[1])
    giant_counts = bag_counts(masked_ids(giant_slot[0, 0], lengths[:, 0]), groups * capacity)
    giant_out = after(tables, small_counts, giant_counts)[:, 0]
    giant_values = exchange(giant_out, "col").reshape(samples, width)

    small_values = small_values.reshape(samples, width)
    pieces = split_bucket_sums(small_counts, small_values, position("row"), lax.axis_size("row"))
    terms = [moved(piece, "row", step) if step else piece for step, piece in enumerate(pieces)]
    size = lax.axis_size("rep")
    distance = size // 2
    while distance:
        keep, send = split_halves(terms, position("rep"), distance)
        terms = [keep, lax.ppermute(send, "rep", [(i, i ^ distance) for i in range(size)])]
        distance //= 2

    packed = packed_bucket_sums(giant_counts, giant_values, capacity, terms)
    arrived = exchange(packed, ("row", "rep"))
    targets = touched_rows[0, :, 0, :].reshape(1, -1)
    new_gw, new_ga, new_sw, new_sa = update(
        targets, arrived, giant_weight[0], giant_accum, small_weight[0], small_accum, capacity
    )
    return (new_gw[None], new_ga, new_sw[None], new_sa)


def solution(mesh):
    placed = (
        P(("row", "rep"), "col", None, None),
        P("col", ("row", "rep"), None, None),
        P("col", None, ("row", "rep"), None),
        P("col", ("row", "rep"), None, None),
        P("col", ("row", "rep"), None, None),
        P("col", ("row", "rep"), None),
        P("col", ("row", "rep")),
        P("col", None, None),
        P("col", None),
    )
    return jax.shard_map(
        body,
        mesh=mesh,
        in_specs=placed,
        out_specs=(
            P("col", ("row", "rep"), None),
            P("col", ("row", "rep")),
            P("col", None, None),
            P("col", None),
        ),
        check_vma=False,
    )
```

```python
import functools

import jax
import jax.numpy as jnp
from jax import lax
from jax.experimental import pallas as pl
from jax.experimental.pallas import tpu as pltpu
from jax.sharding import PartitionSpec as P

LEARN = 0.5
TINY = 1e-08
BF = jnp.bfloat16
F32 = jnp.float32
VMEM_LIMIT = 48 * 1024 * 1024
TAG_ROWS = 16


def masked_ids(ids, lengths):
    live = lax.broadcasted_iota(jnp.int32, ids.shape, 1) < lengths[:, None]
    return jnp.where(live, ids, -1).T


def counts_kernel(ids_ref, out_ref):
    rows, samples = out_ref.shape
    bag = ids_ref.shape[0]
    lanes, tile = 256, 32
    first = pl.program_id(0) * rows
    local = lax.broadcasted_iota(jnp.int32, (tile, lanes), 0)

    @pl.loop(0, samples // lanes)
    def _(chunk):
        at = pl.ds(pl.multiple_of(chunk * lanes, lanes), lanes)
        named = [jnp.broadcast_to(ids_ref[k : k + 1, at], (tile, lanes)) for k in range(bag)]

        @pl.loop(0, rows // tile)
        def _(step):
            bucket = local + (first + step * tile)
            total = jnp.zeros((tile, lanes), jnp.int32)
            for k in range(bag):
                total = total + jnp.where(named[k] == bucket, 1, 0)
            out_ref[pl.ds(pl.multiple_of(step * tile, tile), tile), at] = total.astype(jnp.int8)


def bag_counts(ids, buckets):
    bag, samples = ids.shape
    rows = 256
    return pl.pallas_call(
        counts_kernel,
        grid=(buckets // rows,),
        in_specs=[pl.BlockSpec((bag, samples), lambda i: (0, 0))],
        out_specs=pl.BlockSpec((rows, samples), lambda i: (i, 0)),
        out_shape=jax.ShapeDtypeStruct((buckets, samples), jnp.int8),
        compiler_params=pltpu.CompilerParams(vmem_limit_bytes=VMEM_LIMIT),
        cost_estimate=pl.CostEstimate(
            flops=3 * bag * buckets * samples, bytes_accessed=buckets * samples, transcendentals=0
        ),
    )(ids)


def corner(array):
    lead = (1,) * (array.ndim - 2)
    return pl.BlockSpec(lead + (32, 128), lambda *_: (0,) * array.ndim)


def cut(sums, place, outs):
    piece = outs[0].shape[0]
    for step, out_ref in enumerate(outs):
        member = lax.rem(place + step, len(outs))
        out_ref[...] = sums[pl.ds(pl.multiple_of(member * piece, piece), piece), :]


def split_kernel(place_ref, counts_ref, values_ref, *refs):
    outs, sums = refs[:-1], refs[-1]
    rows = counts_ref.shape[0]
    at = pl.ds(pl.multiple_of(pl.program_id(0) * rows, rows), rows)
    sums[at, :] = jnp.dot(counts_ref[...].astype(BF), values_ref[...], preferred_element_type=F32)

    @pl.when(pl.program_id(0) == pl.num_programs(0) - 1)
    def _():
        cut(sums, place_ref[0], outs)


def halves_kernel(count, distance, place_ref, *refs):
    terms, outs, sums = refs[:count], refs[count:-1], refs[-1]
    total = terms[0][...]
    for term in terms[1:]:
        total = total + term[...]
    sums[...] = total
    cut(sums, lax.div(place_ref[0], distance), outs)


def coded_rows(sums):
    largest = jnp.maximum(jnp.max(jnp.abs(sums), axis=1, keepdims=True), 2.0**-100)
    power = jnp.floor(jnp.log2(largest) + 1e-3) - 14.0
    coded = jnp.clip(jnp.round(sums * jnp.exp2(-power)), -32767.0, 32767.0)
    return coded.astype(jnp.int32).astype(jnp.int16), power


def packed_kernel(capacity, counts_ref, values_ref, *refs):
    terms, (out_ref, small_coded, small_tag) = refs[:-3], refs[-3:]
    lanes = out_ref.shape[2]
    mine, width = small_coded.shape

    def along_lanes(power, first):
        shape = (power.shape[0], lanes)
        row = lax.broadcasted_iota(jnp.int32, shape, 0) + first
        spread = jnp.where(row == lax.broadcasted_iota(jnp.int32, shape, 1), jnp.broadcast_to(power, shape), 0.0)
        return jnp.broadcast_to(jnp.sum(spread, axis=0, keepdims=True), (TAG_ROWS, lanes))

    @pl.when(pl.program_id(0) == 0)
    def _():
        small = terms[0][...]
        for term in terms[1:]:
            small = small + term[...]
        coded, power = coded_rows(small)
        small_coded[...] = coded
        small_tag[...] = along_lanes(power, capacity)

    sums = jnp.dot(counts_ref[...].astype(BF), values_ref[...], preferred_element_type=F32)
    coded, power = coded_rows(sums)
    for block in range(sums.shape[0] // capacity):
        slots = slice(block * capacity, (block + 1) * capacity)
        first = 0
        for piece, count in ((coded[slots, :], capacity), (small_coded[...], mine)):
            for part in range(width // lanes):
                out_ref[block, first : first + count, :] = piece[:, part * lanes : (part + 1) * lanes]
                first += count
        tag = along_lanes(power[slots, :], 0) + small_tag[...]
        out_ref[block, first:, :] = tag.astype(jnp.int32).astype(jnp.int16)


def split_bucket_sums(counts, values, place, members):
    buckets, samples = counts.shape
    width = values.shape[1]
    rows = 512
    piece = (buckets // members, width)
    return pl.pallas_call(
        split_kernel,
        grid=(buckets // rows,),
        in_specs=[
            pl.BlockSpec(memory_space=pltpu.SMEM),
            pl.BlockSpec((rows, samples), lambda i: (i, 0)),
            pl.BlockSpec((samples, width), lambda i: (0, 0)),
        ],
        out_specs=[pl.BlockSpec(piece, lambda i: (0, 0))] * members,
        out_shape=[jax.ShapeDtypeStruct(piece, F32)] * members,
        scratch_shapes=[pltpu.VMEM((buckets, width), F32)],
        compiler_params=pltpu.CompilerParams(vmem_limit_bytes=VMEM_LIMIT),
    )(place, counts, values)


def split_halves(terms, place, distance):
    rows, width = terms[0].shape
    piece = (rows // 2, width)
    return pl.pallas_call(
        functools.partial(halves_kernel, len(terms), distance),
        in_specs=[pl.BlockSpec(memory_space=pltpu.SMEM)] + [pl.BlockSpec(memory_space=pltpu.VMEM)] * len(terms),
        out_specs=[pl.BlockSpec(memory_space=pltpu.VMEM)] * 2,
        out_shape=[jax.ShapeDtypeStruct(piece, F32)] * 2,
        scratch_shapes=[pltpu.VMEM((rows, width), F32)],
        compiler_params=pltpu.CompilerParams(vmem_limit_bytes=VMEM_LIMIT),
    )(place, *terms)


def packed_bucket_sums(counts, values, capacity, terms):
    buckets, samples = counts.shape
    width = values.shape[1]
    rows, lanes = 512, 128
    mine = terms[0].shape[0]
    tall = (capacity + mine) * width // lanes + TAG_ROWS
    whole = pl.BlockSpec(terms[0].shape, lambda i: (0, 0))
    return pl.pallas_call(
        functools.partial(packed_kernel, capacity),
        grid=(buckets // rows,),
        in_specs=[
            pl.BlockSpec((rows, samples), lambda i: (i, 0)),
            pl.BlockSpec((samples, width), lambda i: (0, 0)),
        ]
        + [whole] * len(terms),
        out_specs=pl.BlockSpec((rows // capacity, tall, lanes), lambda i: (i, 0, 0)),
        out_shape=jax.ShapeDtypeStruct((buckets // capacity, tall, lanes), jnp.int16),
        scratch_shapes=[pltpu.VMEM((mine, width), jnp.int16), pltpu.VMEM((TAG_ROWS, lanes), F32)],
        compiler_params=pltpu.CompilerParams(vmem_limit_bytes=VMEM_LIMIT),
    )(counts, values, *terms)


def adagrad_step(weight, accum, grad):
    rows, width = grad.shape
    column = jnp.broadcast_to(accum, (8, rows)).T[:, 0:1]
    total = column + jnp.sum(grad * grad, axis=1, keepdims=True) * (1.0 / width)
    new_weight = weight - grad * (LEARN / (jnp.sqrt(total) + TINY))
    return new_weight, jnp.broadcast_to(total, (rows, 128)).T[0:1, :]


def decoded(coded, scale):
    return coded.astype(jnp.int32).astype(F32) * scale


def update_kernel(
    capacity,
    targets_ref,
    arrived_ref,
    giant_weight_ref,
    giant_accum_ref,
    small_weight_ref,
    small_accum_ref,
    new_giant_weight_ref,
    new_giant_accum_ref,
    new_small_weight_ref,
    new_small_accum_ref,
    parts,
):
    rows, width = giant_weight_ref.shape
    groups, tall, lanes = arrived_ref.shape
    halves = width // lanes
    mine = (tall - TAG_ROWS) // halves - capacity

    def scales(group):
        tag = arrived_ref[group, tall - TAG_ROWS :, :].astype(jnp.int32).astype(F32)
        return jnp.exp2(tag.T[:, 0:1])

    @pl.when(pl.program_id(0) == 0)
    def _():
        for group in range(groups):
            here = slice(group * capacity, (group + 1) * capacity)
            scale = scales(group)[0:capacity]
            for part in range(halves):
                value = decoded(arrived_ref[group, part * capacity : (part + 1) * capacity, :], scale)
                high = value.astype(BF)
                rest = value - high.astype(F32)
                middle = rest.astype(BF)
                low = (rest - middle.astype(F32)).astype(BF)
                for place, piece in enumerate((high, middle, low)):
                    at = place * width + part * lanes
                    parts[here, at : at + lanes] = piece

    sources = groups * capacity
    row = lax.broadcasted_iota(jnp.int32, (rows, sources), 0) + pl.program_id(0) * rows
    hit = jnp.where(jnp.broadcast_to(targets_ref[...], (rows, sources)) == row, 1.0, 0.0).astype(BF)
    product = jnp.dot(hit, parts[...], preferred_element_type=F32)
    grad = product[:, 0:width] + (product[:, width : 2 * width] + product[:, 2 * width :])
    new_weight, new_accum = adagrad_step(giant_weight_ref[...], giant_accum_ref[...], grad)
    new_giant_weight_ref[...] = new_weight
    new_giant_accum_ref[...] = new_accum

    band = lanes // mine
    local_groups = small_weight_ref.shape[0] // mine
    for local in range(0, local_groups, band):
        at = slice(local * mine, (local + band) * mine)
        pieces = []
        for place in range(band):
            group = pl.program_id(0) * local_groups + local + place
            scale = scales(group)[capacity : capacity + mine]
            pair = []
            for part in range(halves):
                first = halves * capacity + part * mine
                pair.append(decoded(arrived_ref[group, first : first + mine, :], scale))
            pieces.append(jnp.concatenate(pair, axis=1))
        grad = jnp.concatenate(pieces, axis=0)
        new_weight, new_accum = adagrad_step(small_weight_ref[at, :], small_accum_ref[:, at], grad)
        new_small_weight_ref[at, :] = new_weight
        new_small_accum_ref[:, at] = new_accum


def update(targets, arrived, giant_weight, giant_accum, small_weight, small_accum, capacity):
    giant_rows, width = giant_weight.shape
    small_rows = small_weight.shape[0]
    sources = targets.shape[1]
    steps = 2

    def blocks(rows):
        return [pl.BlockSpec((rows // steps, width), lambda i: (i, 0)), pl.BlockSpec((1, rows // steps), lambda i: (0, i))]

    def shapes(rows):
        return [jax.ShapeDtypeStruct((rows, width), F32), jax.ShapeDtypeStruct((1, rows), F32)]

    return pl.pallas_call(
        functools.partial(update_kernel, capacity),
        grid=(steps,),
        in_specs=[
            pl.BlockSpec((1, sources), lambda i: (0, 0)),
            pl.BlockSpec(arrived.shape, lambda i: (0, 0, 0)),
        ]
        + blocks(giant_rows)
        + blocks(small_rows),
        out_specs=blocks(giant_rows) + blocks(small_rows),
        out_shape=shapes(giant_rows) + shapes(small_rows),
        scratch_shapes=[pltpu.VMEM((sources, 3 * width), BF)],
        compiler_params=pltpu.CompilerParams(vmem_limit_bytes=VMEM_LIMIT),
    )(targets, arrived, giant_weight, giant_accum, small_weight, small_accum)


def after_kernel(*refs):
    del refs


def after(value, *others):
    place = pl.BlockSpec(memory_space=pl.ANY)
    return pl.pallas_call(
        after_kernel,
        grid=(1,),
        in_specs=[place] + [corner(other) for other in others],
        out_specs=place,
        out_shape=jax.ShapeDtypeStruct(value.shape, value.dtype),
        input_output_aliases={0: 0},
    )(value, *others)


def moved(value, axis, step):
    size = lax.axis_size(axis)
    return lax.ppermute(value, axis, [(i, (i + step) % size) for i in range(size)])


def position(axis):
    return lax.axis_index(axis).astype(jnp.int32).reshape(1)


def body(
    pooled_grad,
    giant_slot,
    touched_rows,
    bag_lengths,
    small_ids,
    giant_weight,
    giant_accum,
    small_weight,
    small_accum,
):
    groups = lax.axis_size("row") * lax.axis_size("rep")
    owners = lax.axis_size("col")
    capacity = touched_rows.shape[3]
    width = small_weight.shape[2]
    samples = giant_slot.shape[2]
    exchange = functools.partial(lax.all_to_all, split_axis=0, concat_axis=0, tiled=True)

    tables = pooled_grad[0].reshape(-1, owners, 2, width).transpose(1, 2, 0, 3)
    small_values = exchange(tables[:, 1], "col")
    lengths = bag_lengths[0, 0]
    small_counts = bag_counts(masked_ids(small_ids[0, 0], lengths[:, 1]), small_weight.shape[1])
    giant_counts = bag_counts(masked_ids(giant_slot[0, 0], lengths[:, 0]), groups * capacity)
    giant_out = after(tables, small_counts, giant_counts)[:, 0]
    giant_values = exchange(giant_out, "col").reshape(samples, width)

    small_values = small_values.reshape(samples, width)
    pieces = split_bucket_sums(small_counts, small_values, position("row"), lax.axis_size("row"))
    terms = [moved(piece, "row", step) if step else piece for step, piece in enumerate(pieces)]
    size = lax.axis_size("rep")
    distance = size // 2
    while distance:
        keep, send = split_halves(terms, position("rep"), distance)
        terms = [keep, lax.ppermute(send, "rep", [(i, i ^ distance) for i in range(size)])]
        distance //= 2

    packed = packed_bucket_sums(giant_counts, giant_values, capacity, terms)
    arrived = exchange(packed, ("row", "rep"))
    targets = touched_rows[0, :, 0, :].reshape(1, -1)
    new_gw, new_ga, new_sw, new_sa = update(
        targets, arrived, giant_weight[0], giant_accum, small_weight[0], small_accum, capacity
    )
    return (new_gw[None], new_ga, new_sw[None], new_sa)


def solution(mesh):
    placed = (
        P(("row", "rep"), "col", None, None),
        P("col", ("row", "rep"), None, None),
        P("col", None, ("row", "rep"), None),
        P("col", ("row", "rep"), None, None),
        P("col", ("row", "rep"), None, None),
        P("col", ("row", "rep"), None),
        P("col", ("row", "rep")),
        P("col", None, None),
        P("col", None),
    )
    return jax.shard_map(
        body,
        mesh=mesh,
        in_specs=placed,
        out_specs=(
            P("col", ("row", "rep"), None),
            P("col", ("row", "rep")),
            P("col", None, None),
            P("col", None),
        ),
        check_vma=False,
    )
```
